256 devices in a mesh: blk: 16 (over y, z_hi, core), win: 16 (over x, z_lo).
Axes of the slice: x: 4, y: 4, z: 8 (z_hi: 2, z_lo: 4; z = z_hi * 4 + z_lo), core: 2. Of those that a mesh axis runs over, the one named last changes fastest.
Arguments:
- spectra: float32 [2, 2048, 16, 4096], P(None, 'win', None, 'blk'), may hold values from -1500 to 1500
- valid: int32 [2048], P('win'), may hold values 0 or 1
Outputs:
- coherence: float32 [2, 16, 4096, 512], P(None, 'win', 'blk')
The draws below stay inside these ranges and needn't reach their ends.
All inputs are finite; a program needn't handle non-finite values. No bound on the sum of `valid` on one device may be relied on, other than what follows from the above.
Results may differ from the reference program's by a relative error of at most 0.0001.
Values sent between devices are 32-bit elements; how exact they have to be, the bound alone decides.
No kernel may reach another device: no remote copies, remote signals or barrier semaphores. Data moves between devices by JAX's collectives and lax.ppermute only.
A program may use at most 128 MiB of HBM per device.

```python
import math
import jax
import jax.numpy as jnp
from jax import lax

CB = 256
F = 16
ROUNDS = 2
NWIN = 2048
CH = 4096
N_BLK = 16


def draw_spectra(key, part):
    key = jax.random.fold_in(key, 1)
    keys = jax.random.split(key, 5)
    shape = (2, NWIN, F, CH)
    noise = jnp.clip(jax.random.normal(keys[0], shape, jnp.float32), -4.0, 4.0)
    top = 10.0
    source = jnp.clip(jax.random.normal(keys[1], (2, NWIN, F, 1), jnp.float32), -4.0, 4.0)
    phase = jax.random.uniform(keys[2], (F, CH), jnp.float32, -math.pi, math.pi)
    cosine = jnp.cos(phase)
    sine = jnp.sin(phase)
    real_part = source[0] * cosine - source[1] * sine
    imag_part = source[0] * sine + source[1] * cosine
    arrival = jnp.stack([real_part, imag_part])
    gain = jnp.exp(jax.random.uniform(keys[3], (1, 1, F, CH), jnp.float32) * math.log(top))
    ramp = jnp.exp(math.log(3.0) * jnp.arange(NWIN, dtype=jnp.float32) / NWIN)
    ramp = ramp * jnp.exp(jax.random.uniform(keys[4], (NWIN,), jnp.float32, -0.35, 0.35))
    return (gain * ramp[None, :, None, None] * (arrival + noise)).astype(jnp.float32)


def plant(entries, rng, smallest, top_value):
    index_at = [jax.random.randint(jax.random.fold_in(rng, axis), (), 0, length) for axis, length in enumerate(entries.shape)]
    widest = entries.shape.index(max(entries.shape))
    beside = index_at[:widest] + [(index_at[widest] + 1) % entries.shape[widest]] + index_at[widest + 1:]
    return entries.at[tuple(index_at)].set(smallest).at[tuple(beside)].set(top_value)


def setup_inputs(seed: int = 0) -> dict:
    streams_of = jax.random.split(jax.random.key(seed), 3)
    return {
        "spectra": draw_spectra(jax.random.fold_in(streams_of[2], 71), 0),
        "valid": plant((jax.random.randint(streams_of[1], (NWIN,), 0, 4) < 3).astype(jnp.int32), jax.random.fold_in(streams_of[1], 1), 0, 1),
    }


def cross_tile(own, other):
    count = own.shape[1]
    left = own.reshape(2 * count, own.shape[2], own.shape[3])
    top = jnp.concatenate([other[0], -other[1]], axis=-1)
    bottom = jnp.concatenate([other[1], other[0]], axis=-1)
    right = jnp.concatenate([top, bottom], axis=0)
    return jnp.einsum('kfi,kfj->fij', left, right, precision=lax.Precision.HIGHEST)

def reference(spectra, valid):
    masked = spectra * valid.astype(jnp.float32)[None, :, None, None]
    energy = lax.optimization_barrier(jnp.sum(masked * masked, axis=(0, 1)))
    scale = 1.0 / jnp.sqrt(energy + 1e-06)
    blocks = N_BLK
    split = masked.reshape(2, NWIN, F, blocks, CB)
    scale_blocks = scale.reshape(F, blocks, CB)
    results = []
    for step in range(ROUNDS):
        partners = jnp.bitwise_xor(jnp.arange(blocks, dtype=jnp.int32), jnp.int32(1 << step))

        def tile(index):
            own = lax.dynamic_index_in_dim(split, index, 3, keepdims=False)
            other = lax.dynamic_index_in_dim(split, partners[index], 3, keepdims=False)
            return cross_tile(own, other)
        tiles = lax.map(tile, jnp.arange(blocks, dtype=jnp.int32))
        tiles = jnp.transpose(tiles, (1, 0, 2, 3))
        partner_scale = jnp.take(scale_blocks, partners, axis=1)
        column_scale = jnp.concatenate([partner_scale, partner_scale], axis=-1)
        tiles = tiles * scale_blocks[:, :, :, None] * column_scale[:, :, None, :]
        results.append(tiles.reshape(F, CH, 2 * CB))
    return jnp.stack(results)
```

```python
import jax
import jax.numpy as jnp
from jax import lax
from jax.experimental import pallas as pl
from jax.experimental.pallas import tpu as pltpu
from jax.sharding import Mesh, PartitionSpec as P

PLANE = ("h", "x", "l")
EXTRA = 8


def sort_kernel(groups, rows, valid_ref, x_ref, out_ref, mask_ref):
    count = valid_ref.shape[1]

    @pl.when((pl.program_id(0) == 0) & (pl.program_id(1) == 0) & (pl.program_id(2) == 0))
    def _():
        keep = valid_ref[...].astype(jnp.float32)
        mask_ref[...] = jnp.broadcast_to(keep, (count, count)).T

    first = pl.multiple_of(pl.program_id(2) * rows, rows)
    mask = mask_ref[pl.ds(first, rows), :x_ref.shape[2]]
    for group in range(groups):
        out_ref[0, group, 0] = x_ref[0, pl.ds(group, rows, stride=groups), :] * mask


def sort_by_bin(spectra, valid):
    parts, windows, bins, chans = spectra.shape
    rows, lanes = 64, 128
    per_half = windows // 2 // rows
    return pl.pallas_call(
        lambda *refs: sort_kernel(bins, rows, *refs),
        out_shape=jax.ShapeDtypeStruct((2, bins, parts, windows // 2, chans), jnp.float32),
        grid=(parts, chans // lanes, windows // rows),
        in_specs=[
            pl.BlockSpec((1, windows), lambda p, c, w: (0, 0)),
            pl.BlockSpec((1, rows * bins, lanes), lambda p, c, w: (p, w, c)),
        ],
        out_specs=pl.BlockSpec(
            (1, bins, 1, rows, lanes),
            lambda p, c, w: (w // per_half, 0, p, w % per_half, c),
        ),
        scratch_shapes=[pltpu.VMEM((windows, windows), jnp.float32)],
    )(valid.reshape(1, windows), spectra.reshape(parts, windows * bins, chans))


def halves(value):
    high = value.astype(jnp.bfloat16)
    return high, (value - high.astype(jnp.float32)).astype(jnp.bfloat16)


def dot(left, right):
    return lax.dot_general(
        left, right, (((0,), (0,)), ((), ())), preferred_element_type=jnp.float32
    )


def tile_kernel(index_ref, left_ref, right_ref, out_ref):
    del index_ref
    chans = left_ref.shape[-1]
    step = pl.program_id(0)

    @pl.when(step == 0)
    def _():
        out_ref[...] = jnp.zeros_like(out_ref)

    left = left_ref[0].reshape(-1, chans)
    right = right_ref[0].reshape(-1, chans)
    group = left_ref.shape[1]
    turned = []
    for at in range(group):
        turned += [-right_ref[0, at, 1], right_ref[0, at, 0]]
    right2 = jnp.concatenate([right, jnp.concatenate(turned, axis=0)], axis=1)
    left_high, left_low = halves(left)
    right_high, right_low = halves(right2)
    out_ref[:chans] += (
        dot(left_high, right_low) + dot(left_low, right_high) + dot(left_high, right_high)
    )
    out_ref[chans:chans + 8, :chans] += jnp.sum((left * left).reshape(-1, 8, chans), axis=0)
    out_ref[chans:chans + 8, chans:] += jnp.sum((right * right).reshape(-1, 8, chans), axis=0)


def cross_tile(left, right, index):
    _, sources, parts, windows, chans = left.shape
    group = 4
    block = (1, group, parts, windows, chans)
    return pl.pallas_call(
        tile_kernel,
        out_shape=jax.ShapeDtypeStruct((chans + EXTRA, 2 * chans), jnp.float32),
        grid_spec=pltpu.PrefetchScalarGridSpec(
            num_scalar_prefetch=1,
            grid=(sources // group,),
            in_specs=[
                pl.BlockSpec(block, lambda k, index: (index[0], k, 0, 0, 0)),
                pl.BlockSpec(block, lambda k, index: (index[1], k, 0, 0, 0)),
            ],
            out_specs=pl.BlockSpec((chans + EXTRA, 2 * chans), lambda k, index: (0, 0)),
        ),
        compiler_params=pltpu.CompilerParams(vmem_limit_bytes=32 * 1024 * 1024),
        cost_estimate=pl.CostEstimate(
            flops=6 * 2 * sources * parts * windows * chans * chans,
            bytes_accessed=2 * 4 * sources * parts * windows * chans,
            transcendentals=0,
        ),
    )(index, left, right)


def weigh_kernel(flag_ref, a_ref, a2_ref, b_ref, b2_ref, out_ref):
    chans = out_ref.shape[2]
    for step, (one, two) in enumerate(((a_ref, a2_ref), (b_ref, b2_ref))):
        energy = jnp.sum(one[chans:] + two[chans:], axis=0, keepdims=True)
        scale = 1.0 / jnp.sqrt(energy + 1e-06)
        across = scale[:, chans:]
        down = jnp.broadcast_to(scale[:, :chans], (chans, chans)).T
        weight = down * across
        real = (one[:chans, :chans] + two[:chans, :chans]) * weight
        imag = (one[:chans, chans:] + two[:chans, chans:]) * weight

        @pl.when(flag_ref[0] == 1)
        def _():
            out_ref[step, 0, :, :chans] = real
            out_ref[step, 0, :, chans:] = imag

        @pl.when(flag_ref[0] == 0)
        def _():
            out_ref[step, 0, :, :chans] = real.T
            out_ref[step, 0, :, chans:] = -imag.T


def weigh(direct, a, a2, b, b2):
    rows, width = a.shape
    chans = width // 2
    return pl.pallas_call(
        weigh_kernel,
        out_shape=jax.ShapeDtypeStruct((2, 1, chans, width), jnp.float32),
        in_specs=[pl.BlockSpec(memory_space=pltpu.SMEM)]
        + [pl.BlockSpec(memory_space=pltpu.VMEM)] * 4,
        out_specs=pl.BlockSpec(memory_space=pltpu.VMEM),
        compiler_params=pltpu.CompilerParams(vmem_limit_bytes=32 * 1024 * 1024),
    )(direct, a, a2, b, b2)


def body(spectra, valid):
    high = lax.axis_index("h")
    core = lax.axis_index("c")
    sent = sort_by_bin(spectra, valid)
    bins, parts, windows, chans = sent.shape[1:]
    sources = 2 * bins
    got = lax.all_to_all(
        sent.reshape(sources, parts, windows, chans), PLANE, 0, 0, tiled=True
    ).reshape(2, bins, parts, windows, chans)
    away = lax.dynamic_index_in_dim(got, 1 - core, 0)
    other = lax.ppermute(away, "c", [(0, 1), (1, 0)])
    far = cross_tile(got, away, jnp.stack([core, jnp.int32(0)]).astype(jnp.int32))
    far_rest = lax.ppermute(far, "h", [(0, 1), (1, 0)])
    near = cross_tile(got, other, jnp.stack([core, jnp.int32(0)]).astype(jnp.int32))
    near_rest = lax.ppermute(near, ("h", "c"), [(1, 3), (2, 0)])
    near_sum = near + near_rest
    direct = high == core
    passed = lax.ppermute(near_sum, ("h", "c"), [(0, 1), (3, 2)])
    near_a = jnp.where(direct, near, passed)
    flag = direct.astype(jnp.int32).reshape(1)
    return weigh(flag, near_a, near_rest, far, far_rest)


def solution(mesh):
    fine = Mesh(mesh.devices.reshape(4, 2, 2, 4, 4), ("y", "h", "c", "x", "l"))
    return jax.shard_map(
        body,
        mesh=fine,
        in_specs=(P(None, ("x", "l"), None, ("y", "h", "c")), P(("x", "l"))),
        out_specs=P(None, ("x", "l"), ("y", "h", "c"), None),
        check_vma=False,
    )
```

```python
import jax
import jax.numpy as jnp
from jax import lax
from jax.experimental import pallas as pl
from jax.experimental.pallas import tpu as pltpu
from jax.sharding import Mesh, PartitionSpec as P

PLANE = ("h", "x", "l")
PIECES = 2
STEPS = 4
EXTRA = 8
VMEM_BYTES = 121 * 512 * 1024


def sort_kernel(valid_ref, x_ref, out_ref, rows_ref, sorted_ref, mask_ref, in_sems, out_sems):
    parts, windows, _, chans = x_ref.shape
    groups = in_sems.shape[1]
    rows, half = windows // groups, windows // 2

    def fetch(part, group):
        span = pl.ds(group * rows, rows)
        return pltpu.make_async_copy(
            x_ref.at[part, span], rows_ref.at[part, span], in_sems.at[part, group]
        )

    def store(part, group):
        side, first = divmod(group * rows, half)
        span = pl.ds(first, rows)
        return pltpu.make_async_copy(
            sorted_ref.at[side, :, part, span],
            out_ref.at[side, :, part, span],
            out_sems.at[part, group],
        )

    steps = [(part, group) for part in range(parts) for group in range(groups)]
    for step in steps:
        fetch(*step).start()
    lanes = mask_ref.shape[1]
    keep = valid_ref[...].astype(jnp.float32)
    mask_ref[...] = jnp.broadcast_to(keep, (lanes, windows)).T
    for part, group in steps:
        fetch(part, group).wait()
        for first in range(group * rows, (group + 1) * rows, 8):
            mask = mask_ref[first:first + 8, :]
            block = jnp.swapaxes(rows_ref[part, first:first + 8], 0, 1)
            side, at = divmod(first, half)
            for lane in range(0, chans, lanes):
                sorted_ref[side, :, part, at:at + 8, lane:lane + lanes] = (
                    block[:, :, lane:lane + lanes] * mask
                )
        store(part, group).start()
    for step in steps:
        store(*step).wait()


def sort_by_bin(spectra, valid):
    parts, windows, bins, chans = spectra.shape
    groups = 4
    shape = (2, bins, parts, windows // 2, chans)
    return pl.pallas_call(
        sort_kernel,
        out_shape=jax.ShapeDtypeStruct(shape, jnp.float32),
        in_specs=[
            pl.BlockSpec(memory_space=pltpu.VMEM),
            pl.BlockSpec(memory_space=pl.ANY),
        ],
        out_specs=pl.BlockSpec(memory_space=pl.ANY),
        scratch_shapes=[
            pltpu.VMEM(spectra.shape, jnp.float32),
            pltpu.VMEM(shape, jnp.float32),
            pltpu.VMEM((windows, 128), jnp.float32),
            pltpu.SemaphoreType.DMA((parts, groups)),
            pltpu.SemaphoreType.DMA((parts, groups)),
        ],
        compiler_params=pltpu.CompilerParams(vmem_limit_bytes=VMEM_BYTES),
    )(valid.reshape(1, windows), spectra)


def halves(value):
    high = value.astype(jnp.bfloat16)
    return high, (value - high.astype(jnp.float32)).astype(jnp.bfloat16)


def dot(left, right):
    return lax.dot_general(
        left, right, (((0,), (0,)), ((), ())), preferred_element_type=jnp.float32
    )


def with_turned(right, windows):
    turned = []
    for at in range(0, right.shape[0], 2 * windows):
        turned += [-right[at + windows:at + 2 * windows], right[at:at + windows]]
    return jnp.concatenate([right, jnp.concatenate(turned, axis=0)], axis=1)


def tile_kernel(cuts, copies, index_ref, left_ref, right_ref, *refs):
    del index_ref
    out_refs = refs[:len(cuts) - 1]
    _, sources, _, windows, chans = left_ref.shape
    first_step = pl.program_id(0) == 0
    if copies:
        refs[-1][...] = right_ref[...]
    left = left_ref[0].reshape(-1, chans)
    right = right_ref[0].reshape(-1, chans)
    left_high, left_low = halves(left)
    right_high, right_low = halves(with_turned(right, windows))
    tile = dot(left_high, right_low) + dot(left_low, right_high) + dot(left_high, right_high)
    energy = jnp.concatenate(
        [jnp.sum((side * side).reshape(-1, EXTRA, chans), axis=0) for side in (left, right)],
        axis=1,
    )

    @pl.when(first_step)
    def _():
        for ref, first, last in zip(out_refs, cuts, cuts[1:]):
            ref[:min(last, chans) - first] = tile[first:min(last, chans)]
        out_refs[-1][chans - cuts[-2]:] = energy

    @pl.when(jnp.logical_not(first_step))
    def _():
        for ref, first, last in zip(out_refs, cuts, cuts[1:]):
            ref[:min(last, chans) - first] += tile[first:min(last, chans)]
        out_refs[-1][chans - cuts[-2]:] += energy


def cross_tile(left, right, index, pieces, same):
    _, sources, parts, windows, chans = left.shape
    cuts = [at * chans // pieces for at in range(pieces)] + [chans + EXTRA]
    group = sources // STEPS
    block = (1, group, parts, windows, chans)
    outs = [
        jax.ShapeDtypeStruct((last - first, 2 * chans), jnp.float32)
        for first, last in zip(cuts, cuts[1:])
    ]
    specs = [pl.BlockSpec(out.shape, lambda k, index: (0, 0)) for out in outs]
    if same:
        outs.append(jax.ShapeDtypeStruct((1,) + right.shape[1:], jnp.float32))
        specs.append(pl.BlockSpec(block, lambda k, index: (0, k, 0, 0, 0)))
    return pl.pallas_call(
        lambda *refs: tile_kernel(cuts, same, *refs),
        out_shape=outs,
        grid_spec=pltpu.PrefetchScalarGridSpec(
            num_scalar_prefetch=1,
            grid=(STEPS,),
            in_specs=[
                pl.BlockSpec(block, lambda k, index: (index[0], k, 0, 0, 0)),
                pl.BlockSpec(block, lambda k, index: (index[1], k, 0, 0, 0)),
            ],
            out_specs=specs,
        ),
        compiler_params=pltpu.CompilerParams(vmem_limit_bytes=32 * 1024 * 1024),
        cost_estimate=pl.CostEstimate(flops=1000, bytes_accessed=1000, transcendentals=0),
    )(index, left, right)


def weigh_kernel(adds, flag_ref, *refs):
    ins, out_ref = refs[:-1], refs[-1]
    chans = out_ref.shape[2]
    direct = flag_ref[0] == 1
    half = len(ins) // adds
    total = jnp.concatenate([sum(ref[...] for ref in ins[at::half]) for at in range(half)], axis=0)
    energy = jnp.sum(total[chans:], axis=0, keepdims=True)
    scale = 1.0 / jnp.sqrt(energy + 1e-06)
    down = jnp.broadcast_to(scale[:, :chans], (chans, chans)).T
    weight = down * scale[:, chans:]
    real = total[:chans, :chans] * weight
    imag = total[:chans, chans:] * weight

    @pl.when(direct)
    def _():
        out_ref[0, 0, :, :chans] = real
        out_ref[0, 0, :, chans:] = imag

    @pl.when(jnp.logical_not(direct))
    def _():
        out_ref[0, 0, :, :chans] = real.T
        out_ref[0, 0, :, chans:] = -imag.T


def weigh(flag, groups, step, onto=None, flops=1000):
    arrays = [piece for group in groups for piece in group]
    width = arrays[0].shape[1]
    kernel = lambda *refs: weigh_kernel(len(groups), *refs)
    extra = []
    if onto is not None:
        kernel = lambda *refs: weigh_kernel(len(groups), refs[0], *refs[2:])
        extra = [onto]
    return pl.pallas_call(
        kernel,
        out_shape=jax.ShapeDtypeStruct((2, 1, width // 2, width), jnp.float32),
        grid=(1,),
        in_specs=[pl.BlockSpec(memory_space=pltpu.SMEM)]
        + [pl.BlockSpec(memory_space=pl.ANY)] * len(extra)
        + [pl.BlockSpec(memory_space=pltpu.VMEM)] * len(arrays),
        out_specs=pl.BlockSpec((1, 1, width // 2, width), lambda k: (step, 0, 0, 0)),
        input_output_aliases={1: 0} if extra else {},
        compiler_params=pltpu.CompilerParams(vmem_limit_bytes=32 * 1024 * 1024),
        cost_estimate=pl.CostEstimate(flops=flops, bytes_accessed=1000, transcendentals=0),
    )(flag, *extra, *arrays)


def body(spectra, valid):
    high = lax.axis_index("h")
    core = lax.axis_index("c")
    index = jnp.stack([core, 1 - core]).astype(jnp.int32)
    index_one = jnp.stack([core, jnp.int32(0)]).astype(jnp.int32)
    flag = (high == core).astype(jnp.int32).reshape(1)
    sent = sort_by_bin(spectra, valid)
    _, bins, parts, windows, chans = sent.shape
    sent = sent.reshape(2 * bins, parts, windows, chans)
    got = lax.all_to_all(sent, PLANE, 0, 0, tiled=True)
    got = got.reshape(2, bins, parts, windows, chans)
    far, away = cross_tile(got, got, index, 1, True)
    other = lax.ppermute(away, "c", [(0, 1), (1, 0)])
    far_rest = lax.ppermute(far, "h", [(0, 1), (1, 0)])
    near = cross_tile(got, other, index_one, PIECES, False)
    near_rest = [lax.ppermute(piece, ("h", "c"), [(1, 3), (2, 0)]) for piece in near]
    near_rest[-1], far_rest = lax.optimization_barrier((near_rest[-1], far_rest))
    passed = [
        lax.ppermute(piece + rest, ("h", "c"), [(0, 1), (3, 2)])
        for piece, rest in zip(near, near_rest)
    ]
    kept = [jnp.where(flag[0] == 1, piece, 0.0) for piece in near]
    out = weigh(flag, ([far], [far_rest]), 1, flops=int(1e9))
    return weigh(flag, (kept, near_rest, passed), 0, out)


def solution(mesh):
    fine = Mesh(mesh.devices.reshape(4, 2, 2, 4, 4), ("y", "h", "c", "x", "l"))
    return jax.shard_map(
        body,
        mesh=fine,
        in_specs=(P(None, ("x", "l"), None, ("y", "h", "c")), P(("x", "l"))),
        out_specs=P(None, ("x", "l"), ("y", "h", "c"), None),
        check_vma=False,
    )
```

```python
import jax
import jax.numpy as jnp
from jax import lax
from jax.experimental import pallas as pl
from jax.experimental.pallas import tpu as pltpu
from jax.sharding import Mesh, PartitionSpec as P

PLANE = ("h", "x", "l")
PIECES = 2
STEPS = 4
SAVED = 8
EXTRA = 8
VMEM_BYTES = 121 * 512 * 1024


def sort_kernel(valid_ref, x_ref, out_ref, rows_ref, sorted_ref, mask_ref, in_sems, out_sems):
    parts, windows, _, chans = x_ref.shape
    groups = in_sems.shape[1]
    rows, half = windows // groups, windows // 2

    def fetch(part, group):
        span = pl.ds(group * rows, rows)
        return pltpu.make_async_copy(
            x_ref.at[part, span], rows_ref.at[part, span], in_sems.at[part, group]
        )

    def store(part, group):
        side, first = divmod(group * rows, half)
        span = pl.ds(first, rows)
        return pltpu.make_async_copy(
            sorted_ref.at[side, :, part, span],
            out_ref.at[side, :, part, span],
            out_sems.at[part, group],
        )

    steps = [(part, group) for part in range(parts) for group in range(groups)]
    for step in steps:
        fetch(*step).start()
    lanes = mask_ref.shape[1]
    keep = valid_ref[...].astype(jnp.float32)
    mask_ref[...] = jnp.broadcast_to(keep, (lanes, windows)).T
    for part, group in steps:
        fetch(part, group).wait()
        for first in range(group * rows, (group + 1) * rows, 8):
            mask = mask_ref[first:first + 8, :]
            block = jnp.swapaxes(rows_ref[part, first:first + 8], 0, 1)
            side, at = divmod(first, half)
            for lane in range(0, chans, lanes):
                sorted_ref[side, :, part, at:at + 8, lane:lane + lanes] = (
                    block[:, :, lane:lane + lanes] * mask
                )
        store(part, group).start()
    for step in steps:
        store(*step).wait()


def sort_by_bin(spectra, valid):
    parts, windows, bins, chans = spectra.shape
    groups = 4
    shape = (2, bins, parts, windows // 2, chans)
    return pl.pallas_call(
        sort_kernel,
        out_shape=jax.ShapeDtypeStruct(shape, jnp.float32),
        in_specs=[
            pl.BlockSpec(memory_space=pltpu.VMEM),
            pl.BlockSpec(memory_space=pl.ANY),
        ],
        out_specs=pl.BlockSpec(memory_space=pl.ANY),
        scratch_shapes=[
            pltpu.VMEM(spectra.shape, jnp.float32),
            pltpu.VMEM(shape, jnp.float32),
            pltpu.VMEM((windows, 128), jnp.float32),
            pltpu.SemaphoreType.DMA((parts, groups)),
            pltpu.SemaphoreType.DMA((parts, groups)),
        ],
        compiler_params=pltpu.CompilerParams(vmem_limit_bytes=VMEM_BYTES),
    )(valid.reshape(1, windows), spectra)


def gather_kernel(valid_ref, x_ref, out_ref, rows_ref, sorted_ref, order_ref, in_sems, out_sems):
    parts, windows, _, chans = x_ref.shape
    groups = in_sems.shape[1]
    size = sorted_ref.shape[3]

    def fetch(part, group):
        span = pl.ds(group * (windows // groups), windows // groups)
        return pltpu.make_async_copy(
            x_ref.at[part, span], rows_ref.at[part, span], in_sems.at[part, group]
        )

    def store(part, side):
        return pltpu.make_async_copy(
            sorted_ref.at[side, :, part], out_ref.at[side, :, part], out_sems.at[part, side]
        )

    for part in range(parts):
        for group in range(groups):
            fetch(part, group).start()

    def clear(at, carry):
        order_ref[at] = 0
        return carry

    def place(at, count):
        order_ref[count] = at
        return count + valid_ref[0, at]

    lax.fori_loop(0, windows, clear, 0, unroll=16)
    count = lax.fori_loop(0, windows, place, jnp.int32(0), unroll=16)
    over = (count > 2 * (size - 1)).astype(jnp.float32)
    for part in range(parts):
        for group in range(groups):
            fetch(part, group).wait()
        for side in range(2):
            held = jnp.minimum(count - side * (size - 1), size - 1)
            for first in range(0, size, 8):
                rows = [
                    rows_ref[part, order_ref[side * (size - 1) + first + at]] for at in range(8)
                ]
                block = jnp.swapaxes(jnp.stack(rows), 0, 1)
                row = lax.broadcasted_iota(jnp.int32, block.shape, 1) + first
                block = jnp.where(row < held, block, 0.0)
                if part == 0 and first + 8 == size:
                    block = jnp.where(row == size - 1, over, block)
                sorted_ref[side, :, part, first:first + 8] = block
            store(part, side).start()
    for part in range(parts):
        for side in range(2):
            store(part, side).wait()


def gather_by_bin(spectra, valid):
    parts, windows, bins, chans = spectra.shape
    groups, size = 2, windows // 2 - SAVED
    shape = (2, bins, parts, size, chans)
    return pl.pallas_call(
        gather_kernel,
        out_shape=jax.ShapeDtypeStruct(shape, jnp.float32),
        in_specs=[
            pl.BlockSpec(memory_space=pltpu.SMEM),
            pl.BlockSpec(memory_space=pl.ANY),
        ],
        out_specs=pl.BlockSpec(memory_space=pl.ANY),
        scratch_shapes=[
            pltpu.VMEM(spectra.shape, jnp.float32),
            pltpu.VMEM(shape, jnp.float32),
            pltpu.SMEM((windows,), jnp.int32),
            pltpu.SemaphoreType.DMA((parts, groups)),
            pltpu.SemaphoreType.DMA((parts, 2)),
        ],
        compiler_params=pltpu.CompilerParams(vmem_limit_bytes=VMEM_BYTES),
    )(valid.reshape(1, windows), spectra)


def halves(value):
    high = value.astype(jnp.bfloat16)
    return high, (value - high.astype(jnp.float32)).astype(jnp.bfloat16)


def dot(left, right):
    return lax.dot_general(
        left, right, (((0,), (0,)), ((), ())), preferred_element_type=jnp.float32
    )


def with_turned(right, windows):
    turned = []
    for at in range(0, right.shape[0], 2 * windows):
        turned += [-right[at + windows:at + 2 * windows], right[at:at + windows]]
    return jnp.concatenate([right, jnp.concatenate(turned, axis=0)], axis=1)


def tile_kernel(cuts, copies, index_ref, left_ref, right_ref, *refs):
    del index_ref
    out_refs = refs[:len(cuts) - 1]
    _, sources, _, windows, chans = left_ref.shape
    first_step = pl.program_id(0) == 0
    if copies:
        refs[-1][...] = right_ref[...]
    left = left_ref[0].reshape(-1, chans)
    right = right_ref[0].reshape(-1, chans)
    left_high, left_low = halves(left)
    right_high, right_low = halves(with_turned(right, windows))
    tile = dot(left_high, right_low) + dot(left_low, right_high) + dot(left_high, right_high)
    energy = jnp.concatenate(
        [jnp.sum((side * side).reshape(-1, EXTRA, chans), axis=0) for side in (left, right)],
        axis=1,
    )

    @pl.when(first_step)
    def _():
        for ref, first, last in zip(out_refs, cuts, cuts[1:]):
            ref[:min(last, chans) - first] = tile[first:min(last, chans)]
        out_refs[-1][chans - cuts[-2]:] = energy

    @pl.when(jnp.logical_not(first_step))
    def _():
        for ref, first, last in zip(out_refs, cuts, cuts[1:]):
            ref[:min(last, chans) - first] += tile[first:min(last, chans)]
        out_refs[-1][chans - cuts[-2]:] += energy


def cross_tile(left, right, index, pieces, same):
    _, sources, parts, windows, chans = left.shape
    cuts = [at * chans // pieces for at in range(pieces)] + [chans + EXTRA]
    group = sources // STEPS
    block = (1, group, parts, windows, chans)
    outs = [
        jax.ShapeDtypeStruct((last - first, 2 * chans), jnp.float32)
        for first, last in zip(cuts, cuts[1:])
    ]
    specs = [pl.BlockSpec(out.shape, lambda k, index: (0, 0)) for out in outs]
    if same:
        outs.append(jax.ShapeDtypeStruct((1,) + right.shape[1:], jnp.float32))
        specs.append(pl.BlockSpec(block, lambda k, index: (0, k, 0, 0, 0)))
    return pl.pallas_call(
        lambda *refs: tile_kernel(cuts, same, *refs),
        out_shape=outs,
        grid_spec=pltpu.PrefetchScalarGridSpec(
            num_scalar_prefetch=1,
            grid=(STEPS,),
            in_specs=[
                pl.BlockSpec(block, lambda k, index: (index[0], k, 0, 0, 0)),
                pl.BlockSpec(block, lambda k, index: (index[1], k, 0, 0, 0)),
            ],
            out_specs=specs,
        ),
        compiler_params=pltpu.CompilerParams(vmem_limit_bytes=32 * 1024 * 1024),
        cost_estimate=pl.CostEstimate(flops=1000, bytes_accessed=1000, transcendentals=0),
    )(index, left, right)


def weigh_kernel(adds, flag_ref, *refs):
    ins, out_ref = refs[:-1], refs[-1]
    chans = out_ref.shape[2]
    direct = flag_ref[0] == 1
    half = len(ins) // adds
    total = jnp.concatenate([sum(ref[...] for ref in ins[at::half]) for at in range(half)], axis=0)
    energy = jnp.sum(total[chans:], axis=0, keepdims=True)
    scale = 1.0 / jnp.sqrt(energy + 1e-06)
    down = jnp.broadcast_to(scale[:, :chans], (chans, chans)).T
    weight = down * scale[:, chans:]
    real = total[:chans, :chans] * weight
    imag = total[:chans, chans:] * weight

    @pl.when(direct)
    def _():
        out_ref[0, 0, :, :chans] = real
        out_ref[0, 0, :, chans:] = imag

    @pl.when(jnp.logical_not(direct))
    def _():
        out_ref[0, 0, :, :chans] = real.T
        out_ref[0, 0, :, chans:] = -imag.T


def weigh(flag, groups, step, onto=None, flops=1000):
    arrays = [piece for group in groups for piece in group]
    width = arrays[0].shape[1]
    kernel = lambda *refs: weigh_kernel(len(groups), *refs)
    extra = []
    if onto is not None:
        kernel = lambda *refs: weigh_kernel(len(groups), refs[0], *refs[2:])
        extra = [onto]
    return pl.pallas_call(
        kernel,
        out_shape=jax.ShapeDtypeStruct((2, 1, width // 2, width), jnp.float32),
        grid=(1,),
        in_specs=[pl.BlockSpec(memory_space=pltpu.SMEM)]
        + [pl.BlockSpec(memory_space=pl.ANY)] * len(extra)
        + [pl.BlockSpec(memory_space=pltpu.VMEM)] * len(arrays),
        out_specs=pl.BlockSpec((1, 1, width // 2, width), lambda k: (step, 0, 0, 0)),
        input_output_aliases={1: 0} if extra else {},
        compiler_params=pltpu.CompilerParams(vmem_limit_bytes=32 * 1024 * 1024),
        cost_estimate=pl.CostEstimate(flops=flops, bytes_accessed=1000, transcendentals=0),
    )(flag, *extra, *arrays)


def coherence(sent):
    high = lax.axis_index("h")
    core = lax.axis_index("c")
    index = jnp.stack([core, 1 - core]).astype(jnp.int32)
    index_one = jnp.stack([core, jnp.int32(0)]).astype(jnp.int32)
    flag = (high == core).astype(jnp.int32).reshape(1)
    _, bins, parts, windows, chans = sent.shape
    sent = sent.reshape(2 * bins, parts, windows, chans)
    got = lax.all_to_all(sent, PLANE, 0, 0, tiled=True)
    got = got.reshape(2, bins, parts, windows, chans)
    far, away = cross_tile(got, got, index, 1, True)
    other = lax.ppermute(away, "c", [(0, 1), (1, 0)])
    far_rest = lax.ppermute(far, "h", [(0, 1), (1, 0)])
    near = cross_tile(got, other, index_one, PIECES, False)
    near_rest = [lax.ppermute(piece, ("h", "c"), [(1, 3), (2, 0)]) for piece in near]
    near_rest[-1], far_rest = lax.optimization_barrier((near_rest[-1], far_rest))
    passed = [
        lax.ppermute(piece + rest, ("h", "c"), [(0, 1), (3, 2)])
        for piece, rest in zip(near, near_rest)
    ]
    kept = [jnp.where(flag[0] == 1, piece, 0.0) for piece in near]
    out = weigh(flag, ([far], [far_rest]), 1, flops=int(1e9))
    return weigh(flag, (kept, near_rest, passed), 0, out), jnp.max(got[:, :, 0, -1, :128]) > 0


def body(spectra, valid):
    quick, over = coherence(gather_by_bin(spectra, valid))
    return lax.cond(
        over,
        lambda: coherence(sort_by_bin(spectra, valid))[0],
        lambda: quick,
    )


def solution(mesh):
    fine = Mesh(mesh.devices.reshape(4, 2, 2, 4, 4), ("y", "h", "c", "x", "l"))
    return jax.shard_map(
        body,
        mesh=fine,
        in_specs=(P(None, ("x", "l"), None, ("y", "h", "c")), P(("x", "l"))),
        out_specs=P(None, ("x", "l"), ("y", "h", "c"), None),
        check_vma=False,
    )
```

```python
import jax
import jax.numpy as jnp
from jax import lax
from jax.experimental import pallas as pl
from jax.experimental.pallas import tpu as pltpu
from jax.sharding import Mesh, PartitionSpec as P

PLANE = ("h", "x", "l")
FAR_CUTS = (160,)
NEAR_CUTS = (128,)
STEPS = 2
SAVED = 8
MARK = 1e6
EXTRA = 8
VMEM_BYTES = 121 * 512 * 1024


def sort_kernel(valid_ref, x_ref, out_ref, rows_ref, sorted_ref, mask_ref, in_sems, out_sems):
    parts, windows, _, chans = x_ref.shape
    groups = in_sems.shape[1]
    rows, half = windows // groups, windows // 2

    def fetch(part, group):
        span = pl.ds(group * rows, rows)
        return pltpu.make_async_copy(
            x_ref.at[part, span], rows_ref.at[part, span], in_sems.at[part, group]
        )

    def store(part, group):
        side, first = divmod(group * rows, half)
        span = pl.ds(first, rows)
        return pltpu.make_async_copy(
            sorted_ref.at[side, :, part, span],
            out_ref.at[side, :, part, span],
            out_sems.at[part, group],
        )

    steps = [(part, group) for part in range(parts) for group in range(groups)]
    for step in steps:
        fetch(*step).start()
    lanes = mask_ref.shape[1]
    keep = valid_ref[...].astype(jnp.float32)
    mask_ref[...] = jnp.broadcast_to(keep, (lanes, windows)).T
    for part, group in steps:
        fetch(part, group).wait()
        for first in range(group * rows, (group + 1) * rows, 8):
            mask = mask_ref[first:first + 8, :]
            block = jnp.swapaxes(rows_ref[part, first:first + 8], 0, 1)
            side, at = divmod(first, half)
            for lane in range(0, chans, lanes):
                sorted_ref[side, :, part, at:at + 8, lane:lane + lanes] = (
                    block[:, :, lane:lane + lanes] * mask
                )
        store(part, group).start()
    for step in steps:
        store(*step).wait()


def sort_by_bin(spectra, valid):
    parts, windows, bins, chans = spectra.shape
    groups = 4
    shape = (2, bins, parts, windows // 2, chans)
    return pl.pallas_call(
        sort_kernel,
        out_shape=jax.ShapeDtypeStruct(shape, jnp.float32),
        in_specs=[
            pl.BlockSpec(memory_space=pltpu.VMEM),
            pl.BlockSpec(memory_space=pl.ANY),
        ],
        out_specs=pl.BlockSpec(memory_space=pl.ANY),
        scratch_shapes=[
            pltpu.VMEM(spectra.shape, jnp.float32),
            pltpu.VMEM(shape, jnp.float32),
            pltpu.VMEM((windows, 128), jnp.float32),
            pltpu.SemaphoreType.DMA((parts, groups)),
            pltpu.SemaphoreType.DMA((parts, groups)),
        ],
        compiler_params=pltpu.CompilerParams(vmem_limit_bytes=VMEM_BYTES),
    )(valid.reshape(1, windows), spectra)


def gather_kernel(valid_ref, x_ref, out_ref, rows_ref, sorted_ref, order_ref, in_sems, out_sems):
    parts, windows, _, chans = x_ref.shape
    groups = in_sems.shape[1]
    size = sorted_ref.shape[3]

    def fetch(part, group):
        span = pl.ds(group * (windows // groups), windows // groups)
        return pltpu.make_async_copy(
            x_ref.at[part, span], rows_ref.at[part, span], in_sems.at[part, group]
        )

    def store(part, side):
        return pltpu.make_async_copy(
            sorted_ref.at[side, :, part], out_ref.at[side, :, part], out_sems.at[part, side]
        )

    for part in range(parts):
        for group in range(groups):
            fetch(part, group).start()

    def clear(at, carry):
        order_ref[at] = 0
        return carry

    def place(at, count):
        order_ref[count] = at
        return count + valid_ref[0, at]

    lax.fori_loop(0, windows, clear, 0, unroll=16)
    count = lax.fori_loop(0, windows, place, jnp.int32(0), unroll=16)
    mark = jnp.where(count > 2 * size, MARK, 0.0)
    for part in range(parts):
        for group in range(groups):
            fetch(part, group).wait()
        for side in range(2):
            held = count - side * size
            for first in range(0, size, 8):
                rows = [
                    rows_ref[part, order_ref[side * size + first + at]] for at in range(8)
                ]
                block = jnp.swapaxes(jnp.stack(rows), 0, 1)
                row = lax.broadcasted_iota(jnp.int32, block.shape, 1) + first
                block = jnp.where(row < held, block, 0.0)
                if part == 0 and first + 8 == size:
                    block += jnp.where(row == size - 1, mark, 0.0)
                sorted_ref[side, :, part, first:first + 8] = block
            store(part, side).start()
    for part in range(parts):
        for side in range(2):
            store(part, side).wait()


def gather_by_bin(spectra, valid):
    parts, windows, bins, chans = spectra.shape
    groups, size = 2, windows // 2 - SAVED
    shape = (2, bins, parts, size, chans)
    return pl.pallas_call(
        gather_kernel,
        out_shape=jax.ShapeDtypeStruct(shape, jnp.float32),
        in_specs=[
            pl.BlockSpec(memory_space=pltpu.SMEM),
            pl.BlockSpec(memory_space=pl.ANY),
        ],
        out_specs=pl.BlockSpec(memory_space=pl.ANY),
        scratch_shapes=[
            pltpu.VMEM(spectra.shape, jnp.float32),
            pltpu.VMEM(shape, jnp.float32),
            pltpu.SMEM((windows,), jnp.int32),
            pltpu.SemaphoreType.DMA((parts, groups)),
            pltpu.SemaphoreType.DMA((parts, 2)),
        ],
        compiler_params=pltpu.CompilerParams(vmem_limit_bytes=VMEM_BYTES),
    )(valid.reshape(1, windows), spectra)


def halves(value):
    high = value.astype(jnp.bfloat16)
    return high, (value - high.astype(jnp.float32)).astype(jnp.bfloat16)


def dot(left, right):
    return lax.dot_general(
        left, right, (((0,), (0,)), ((), ())), preferred_element_type=jnp.float32
    )


def with_turned(right, windows):
    turned = []
    for at in range(0, right.shape[0], 2 * windows):
        turned += [-right[at + windows:at + 2 * windows], right[at:at + windows]]
    return jnp.concatenate([right, jnp.concatenate(turned, axis=0)], axis=1)


def tile_kernel(cuts, copies, index_ref, left_ref, right_ref, *refs):
    del index_ref
    out_refs = refs[:len(cuts) - 1]
    _, sources, _, windows, chans = left_ref.shape
    first_step = pl.program_id(0) == 0
    if copies:
        refs[-2][...] = right_ref[...]
        last_slot = left_ref.shape[3] - 1
        largest = jnp.maximum(left_ref[0, :, 0, last_slot], right_ref[0, :, 0, last_slot])
        over = (jnp.max(largest[:, :128]) > 0.5 * MARK).astype(jnp.int32)
        refs[-1][0] = jnp.where(first_step, over, jnp.maximum(refs[-1][0], over))
    left = left_ref[0].reshape(-1, chans)
    right = right_ref[0].reshape(-1, chans)
    left_high, left_low = halves(left)
    right_high, right_low = halves(with_turned(right, windows))
    tile = dot(left_high, right_low) + dot(left_low, right_high) + dot(left_high, right_high)
    energy = jnp.concatenate(
        [jnp.sum((side * side).reshape(-1, EXTRA, chans), axis=0) for side in (left, right)],
        axis=1,
    )

    @pl.when(first_step)
    def _():
        for ref, first, last in zip(out_refs, cuts, cuts[1:]):
            ref[:min(last, chans) - first] = tile[first:min(last, chans)]
        out_refs[-1][chans - cuts[-2]:] = energy

    @pl.when(jnp.logical_not(first_step))
    def _():
        for ref, first, last in zip(out_refs, cuts, cuts[1:]):
            ref[:min(last, chans) - first] += tile[first:min(last, chans)]
        out_refs[-1][chans - cuts[-2]:] += energy


def cross_tile(left, right, index, cuts, same):
    _, sources, parts, windows, chans = left.shape
    cuts = [0, *cuts, chans + EXTRA]
    group = sources // STEPS
    block = (1, group, parts, windows, chans)
    outs = [
        jax.ShapeDtypeStruct((last - first, 2 * chans), jnp.float32)
        for first, last in zip(cuts, cuts[1:])
    ]
    specs = [pl.BlockSpec(out.shape, lambda k, index: (0, 0)) for out in outs]
    if same:
        outs.append(jax.ShapeDtypeStruct((1,) + right.shape[1:], jnp.float32))
        specs.append(pl.BlockSpec(block, lambda k, index: (0, k, 0, 0, 0)))
        outs.append(jax.ShapeDtypeStruct((1,), jnp.int32))
        specs.append(pl.BlockSpec(memory_space=pltpu.SMEM))
    return pl.pallas_call(
        lambda *refs: tile_kernel(cuts, same, *refs),
        out_shape=outs,
        grid_spec=pltpu.PrefetchScalarGridSpec(
            num_scalar_prefetch=1,
            grid=(STEPS,),
            in_specs=[
                pl.BlockSpec(block, lambda k, index: (index[0], k, 0, 0, 0)),
                pl.BlockSpec(block, lambda k, index: (index[1], k, 0, 0, 0)),
            ],
            out_specs=specs,
        ),
        compiler_params=pltpu.CompilerParams(vmem_limit_bytes=32 * 1024 * 1024),
        cost_estimate=pl.CostEstimate(flops=1000, bytes_accessed=1000, transcendentals=0),
    )(index, left, right)


def weigh_kernel(adds, flag_ref, *refs):
    ins, out_ref = refs[:-1], refs[-1]
    chans = out_ref.shape[2]
    direct = flag_ref[0] == 1
    half = len(ins) // adds
    total = jnp.concatenate([sum(ref[...] for ref in ins[at::half]) for at in range(half)], axis=0)
    energy = jnp.sum(total[chans:], axis=0, keepdims=True)
    scale = 1.0 / jnp.sqrt(energy + 1e-06)
    down = jnp.broadcast_to(scale[:, :chans], (chans, chans)).T
    weight = down * scale[:, chans:]
    real = total[:chans, :chans] * weight
    imag = total[:chans, chans:] * weight

    @pl.when(direct)
    def _():
        out_ref[0, 0, :, :chans] = real
        out_ref[0, 0, :, chans:] = imag

    @pl.when(jnp.logical_not(direct))
    def _():
        out_ref[0, 0, :, :chans] = real.T
        out_ref[0, 0, :, chans:] = -imag.T


def weigh(flag, groups, step, onto=None, flops=1000):
    arrays = [piece for group in groups for piece in group]
    width = arrays[0].shape[1]
    kernel = lambda *refs: weigh_kernel(len(groups), *refs)
    extra = []
    if onto is not None:
        kernel = lambda *refs: weigh_kernel(len(groups), refs[0], *refs[2:])
        extra = [onto]
    return pl.pallas_call(
        kernel,
        out_shape=jax.ShapeDtypeStruct((2, 1, width // 2, width), jnp.float32),
        grid=(1,),
        in_specs=[pl.BlockSpec(memory_space=pltpu.SMEM)]
        + [pl.BlockSpec(memory_space=pl.ANY)] * len(extra)
        + [pl.BlockSpec(memory_space=pltpu.VMEM)] * len(arrays),
        out_specs=pl.BlockSpec((1, 1, width // 2, width), lambda k: (step, 0, 0, 0)),
        input_output_aliases={1: 0} if extra else {},
        compiler_params=pltpu.CompilerParams(vmem_limit_bytes=32 * 1024 * 1024),
        cost_estimate=pl.CostEstimate(flops=flops, bytes_accessed=1000, transcendentals=0),
    )(flag, *extra, *arrays)


def coherence(sent):
    high = lax.axis_index("h")
    core = lax.axis_index("c")
    index = jnp.stack([core, 1 - core]).astype(jnp.int32)
    index_one = jnp.stack([core, jnp.int32(0)]).astype(jnp.int32)
    flag = (high == core).astype(jnp.int32).reshape(1)
    _, bins, parts, windows, chans = sent.shape
    sent = sent.reshape(2 * bins, parts, windows, chans)
    got = lax.all_to_all(sent, PLANE, 0, 0, tiled=True)
    got = got.reshape(2, bins, parts, windows, chans)
    *far, away, over = cross_tile(got, got, index, FAR_CUTS, True)
    other = lax.ppermute(away, "c", [(0, 1), (1, 0)])
    far_rest = [lax.ppermute(piece, "h", [(0, 1), (1, 0)]) for piece in far]
    near = cross_tile(got, other, index_one, NEAR_CUTS, False)
    near_rest = [lax.ppermute(piece, ("h", "c"), [(1, 3), (2, 0)]) for piece in near]
    near_rest[-1], far_rest[0] = lax.optimization_barrier((near_rest[-1], far_rest[0]))
    passed = [
        lax.ppermute(piece + rest, ("h", "c"), [(0, 1), (3, 2)])
        for piece, rest in zip(near, near_rest)
    ]
    kept = [jnp.where(flag[0] == 1, piece, 0.0) for piece in near]
    out = weigh(flag, (far, far_rest), 1, flops=int(1e9))
    return weigh(flag, (kept, near_rest, passed), 0, out), over[0] > 0


def body(spectra, valid):
    quick, over = coherence(gather_by_bin(spectra, valid))
    return lax.cond(
        over,
        lambda: coherence(sort_by_bin(spectra, valid))[0],
        lambda: quick,
    )


def solution(mesh):
    fine = Mesh(mesh.devices.reshape(4, 2, 2, 4, 4), ("y", "h", "c", "x", "l"))
    return jax.shard_map(
        body,
        mesh=fine,
        in_specs=(P(None, ("x", "l"), None, ("y", "h", "c")), P(("x", "l"))),
        out_specs=P(None, ("x", "l"), ("y", "h", "c"), None),
        check_vma=False,
    )
```

```python
import jax
import jax.numpy as jnp
from jax import lax
from jax.experimental import pallas as pl
from jax.experimental.pallas import tpu as pltpu
from jax.sharding import Mesh, PartitionSpec as P

PLANE = ("h", "x", "l")
FAR_CUTS = (144,)
NEAR_CUTS = (128,)
STEPS = 1
SAVED = 8
MARK = 1e6
EXTRA = 8
VMEM_BYTES = 121 * 512 * 1024


def sort_kernel(valid_ref, x_ref, out_ref, rows_ref, sorted_ref, mask_ref, in_sems, out_sems):
    parts, windows, _, chans = x_ref.shape
    groups = in_sems.shape[1]
    rows, half = windows // groups, windows // 2

    def fetch(part, group):
        span = pl.ds(group * rows, rows)
        return pltpu.make_async_copy(
            x_ref.at[part, span], rows_ref.at[part, span], in_sems.at[part, group]
        )

    def store(part, group):
        side, first = divmod(group * rows, half)
        span = pl.ds(first, rows)
        return pltpu.make_async_copy(
            sorted_ref.at[side, :, part, span],
            out_ref.at[side, :, part, span],
            out_sems.at[part, group],
        )

    steps = [(part, group) for part in range(parts) for group in range(groups)]
    for step in steps:
        fetch(*step).start()
    lanes = mask_ref.shape[1]
    keep = valid_ref[...].astype(jnp.float32)
    mask_ref[...] = jnp.broadcast_to(keep, (lanes, windows)).T
    for part, group in steps:
        fetch(part, group).wait()
        for first in range(group * rows, (group + 1) * rows, 8):
            mask = mask_ref[first:first + 8, :]
            block = jnp.swapaxes(rows_ref[part, first:first + 8], 0, 1)
            side, at = divmod(first, half)
            for lane in range(0, chans, lanes):
                sorted_ref[side, :, part, at:at + 8, lane:lane + lanes] = (
                    block[:, :, lane:lane + lanes] * mask
                )
        store(part, group).start()
    for step in steps:
        store(*step).wait()


def sort_by_bin(spectra, valid):
    parts, windows, bins, chans = spectra.shape
    groups = 4
    shape = (2, bins, parts, windows // 2, chans)
    return pl.pallas_call(
        sort_kernel,
        out_shape=jax.ShapeDtypeStruct(shape, jnp.float32),
        in_specs=[
            pl.BlockSpec(memory_space=pltpu.VMEM),
            pl.BlockSpec(memory_space=pl.ANY),
        ],
        out_specs=pl.BlockSpec(memory_space=pl.ANY),
        scratch_shapes=[
            pltpu.VMEM(spectra.shape, jnp.float32),
            pltpu.VMEM(shape, jnp.float32),
            pltpu.VMEM((windows, 128), jnp.float32),
            pltpu.SemaphoreType.DMA((parts, groups)),
            pltpu.SemaphoreType.DMA((parts, groups)),
        ],
        compiler_params=pltpu.CompilerParams(vmem_limit_bytes=VMEM_BYTES),
    )(valid.reshape(1, windows), spectra)


def gather_kernel(valid_ref, x_ref, out_ref, rows_ref, sorted_ref, order_ref, in_sems, out_sems):
    parts, windows, _, chans = x_ref.shape
    groups = in_sems.shape[1]
    size = sorted_ref.shape[3]

    def fetch(part, group):
        span = pl.ds(group * (windows // groups), windows // groups)
        return pltpu.make_async_copy(
            x_ref.at[part, span], rows_ref.at[part, span], in_sems.at[part, group]
        )

    def store(part, side):
        return pltpu.make_async_copy(
            sorted_ref.at[side, :, part], out_ref.at[side, :, part], out_sems.at[part, side]
        )

    for part in range(parts):
        for group in range(groups):
            fetch(part, group).start()

    def place(at, count):
        order_ref[count] = at
        return count + valid_ref[0, at]

    count = lax.fori_loop(0, windows, place, jnp.int32(0), unroll=16)
    def pick(slot):
        return jnp.where(slot < count, order_ref[slot], 0)

    mark = jnp.where(count > 2 * size, MARK, 0.0)
    for part in range(parts):
        for group in range(groups):
            fetch(part, group).wait()
        for side in range(2):
            held = count - side * size
            for first in range(0, size, 8):
                rows = [
                    rows_ref[part, pick(side * size + first + at)] for at in range(8)
                ]
                block = jnp.swapaxes(jnp.stack(rows), 0, 1)
                row = lax.broadcasted_iota(jnp.int32, block.shape, 1) + first
                block = jnp.where(row < held, block, 0.0)
                if part == 0 and first + 8 == size:
                    block += jnp.where(row == size - 1, mark, 0.0)
                sorted_ref[side, :, part, first:first + 8] = block
            store(part, side).start()
    for part in range(parts):
        for side in range(2):
            store(part, side).wait()


def gather_by_bin(spectra, valid):
    parts, windows, bins, chans = spectra.shape
    groups, size = 2, windows // 2 - SAVED
    shape = (2, bins, parts, size, chans)
    return pl.pallas_call(
        gather_kernel,
        out_shape=jax.ShapeDtypeStruct(shape, jnp.float32),
        in_specs=[
            pl.BlockSpec(memory_space=pltpu.SMEM),
            pl.BlockSpec(memory_space=pl.ANY),
        ],
        out_specs=pl.BlockSpec(memory_space=pl.ANY),
        scratch_shapes=[
            pltpu.VMEM(spectra.shape, jnp.float32),
            pltpu.VMEM(shape, jnp.float32),
            pltpu.SMEM((windows,), jnp.int32),
            pltpu.SemaphoreType.DMA((parts, groups)),
            pltpu.SemaphoreType.DMA((parts, 2)),
        ],
        compiler_params=pltpu.CompilerParams(vmem_limit_bytes=VMEM_BYTES),
    )(valid.reshape(1, windows), spectra)


def halves(value):
    high = value.astype(jnp.bfloat16)
    return high, (value - high.astype(jnp.float32)).astype(jnp.bfloat16)


def dot(left, right):
    return lax.dot_general(
        left, right, (((0,), (0,)), ((), ())), preferred_element_type=jnp.float32
    )


def with_turned(right, windows):
    turned = []
    for at in range(0, right.shape[0], 2 * windows):
        turned += [-right[at + windows:at + 2 * windows], right[at:at + windows]]
    return jnp.concatenate([right, jnp.concatenate(turned, axis=0)], axis=1)


def tile_kernel(cuts, copies, index_ref, left_ref, right_ref, *refs):
    del index_ref
    out_refs = refs[:len(cuts) - 1]
    _, sources, _, windows, chans = left_ref.shape
    first_step = pl.program_id(0) == 0
    if copies:
        refs[-2][...] = right_ref[...]
        last_slot = left_ref.shape[3] - 1
        largest = jnp.maximum(left_ref[0, :, 0, last_slot], right_ref[0, :, 0, last_slot])
        over = (jnp.max(largest[:, :128]) > 0.5 * MARK).astype(jnp.int32)
        refs[-1][0] = jnp.where(first_step, over, jnp.maximum(refs[-1][0], over))
    left = left_ref[0].reshape(-1, chans)
    right = right_ref[0].reshape(-1, chans)
    left_high, left_low = halves(left)
    right_high, right_low = halves(with_turned(right, windows))
    tile = dot(left_high, right_low) + dot(left_low, right_high) + dot(left_high, right_high)
    energy = jnp.concatenate(
        [jnp.sum((side * side).reshape(-1, EXTRA, chans), axis=0) for side in (left, right)],
        axis=1,
    )

    @pl.when(first_step)
    def _():
        for ref, first, last in zip(out_refs, cuts, cuts[1:]):
            ref[:min(last, chans) - first] = tile[first:min(last, chans)]
        out_refs[-1][chans - cuts[-2]:] = energy

    @pl.when(jnp.logical_not(first_step))
    def _():
        for ref, first, last in zip(out_refs, cuts, cuts[1:]):
            ref[:min(last, chans) - first] += tile[first:min(last, chans)]
        out_refs[-1][chans - cuts[-2]:] += energy


def cross_tile(left, right, index, cuts, same):
    _, sources, parts, windows, chans = left.shape
    cuts = [0, *cuts, chans + EXTRA]
    group = sources // STEPS
    block = (1, group, parts, windows, chans)
    outs = [
        jax.ShapeDtypeStruct((last - first, 2 * chans), jnp.float32)
        for first, last in zip(cuts, cuts[1:])
    ]
    specs = [pl.BlockSpec(out.shape, lambda k, index: (0, 0)) for out in outs]
    if same:
        outs.append(jax.ShapeDtypeStruct((1,) + right.shape[1:], jnp.float32))
        specs.append(pl.BlockSpec(block, lambda k, index: (0, k, 0, 0, 0)))
        outs.append(jax.ShapeDtypeStruct((1,), jnp.int32))
        specs.append(pl.BlockSpec(memory_space=pltpu.SMEM))
    return pl.pallas_call(
        lambda *refs: tile_kernel(cuts, same, *refs),
        out_shape=outs,
        grid_spec=pltpu.PrefetchScalarGridSpec(
            num_scalar_prefetch=1,
            grid=(STEPS,),
            in_specs=[
                pl.BlockSpec(block, lambda k, index: (index[0], k, 0, 0, 0)),
                pl.BlockSpec(block, lambda k, index: (index[1], k, 0, 0, 0)),
            ],
            out_specs=specs,
        ),
        compiler_params=pltpu.CompilerParams(vmem_limit_bytes=32 * 1024 * 1024),
        cost_estimate=pl.CostEstimate(flops=1000, bytes_accessed=1000, transcendentals=0),
    )(index, left, right)


def weigh_kernel(adds, flag_ref, *refs):
    ins, out_ref = refs[:-1], refs[-1]
    chans = out_ref.shape[2]
    direct = flag_ref[0] == 1
    half = len(ins) // adds
    total = jnp.concatenate([sum(ref[...] for ref in ins[at::half]) for at in range(half)], axis=0)
    energy = jnp.sum(total[chans:], axis=0, keepdims=True)
    scale = 1.0 / jnp.sqrt(energy + 1e-06)
    down = jnp.broadcast_to(scale[:, :chans], (chans, chans)).T
    weight = down * scale[:, chans:]
    real = total[:chans, :chans] * weight
    imag = total[:chans, chans:] * weight

    @pl.when(direct)
    def _():
        out_ref[0, 0, :, :chans] = real
        out_ref[0, 0, :, chans:] = imag

    @pl.when(jnp.logical_not(direct))
    def _():
        out_ref[0, 0, :, :chans] = real.T
        out_ref[0, 0, :, chans:] = -imag.T


def weigh(flag, groups, step, onto=None, flops=1000):
    arrays = [piece for group in groups for piece in group]
    width = arrays[0].shape[1]
    kernel = lambda *refs: weigh_kernel(len(groups), *refs)
    extra = []
    if onto is not None:
        kernel = lambda *refs: weigh_kernel(len(groups), refs[0], *refs[2:])
        extra = [onto]
    return pl.pallas_call(
        kernel,
        out_shape=jax.ShapeDtypeStruct((2, 1, width // 2, width), jnp.float32),
        grid=(1,),
        in_specs=[pl.BlockSpec(memory_space=pltpu.SMEM)]
        + [pl.BlockSpec(memory_space=pl.ANY)] * len(extra)
        + [pl.BlockSpec(memory_space=pltpu.VMEM)] * len(arrays),
        out_specs=pl.BlockSpec((1, 1, width // 2, width), lambda k: (step, 0, 0, 0)),
        input_output_aliases={1: 0} if extra else {},
        compiler_params=pltpu.CompilerParams(vmem_limit_bytes=32 * 1024 * 1024),
        cost_estimate=pl.CostEstimate(flops=flops, bytes_accessed=1000, transcendentals=0),
    )(flag, *extra, *arrays)


def coherence(sent):
    high = lax.axis_index("h")
    core = lax.axis_index("c")
    index = jnp.stack([core, 1 - core]).astype(jnp.int32)
    index_one = jnp.stack([core, jnp.int32(0)]).astype(jnp.int32)
    flag = (high == core).astype(jnp.int32).reshape(1)
    _, bins, parts, windows, chans = sent.shape
    sent = sent.reshape(2 * bins, parts, windows, chans)
    got = lax.all_to_all(sent, PLANE, 0, 0, tiled=True)
    got = got.reshape(2, bins, parts, windows, chans)
    *far, away, over = cross_tile(got, got, index, FAR_CUTS, True)
    other = lax.ppermute(away, "c", [(0, 1), (1, 0)])
    far_rest = [lax.ppermute(piece, "h", [(0, 1), (1, 0)]) for piece in far]
    near = cross_tile(got, other, index_one, NEAR_CUTS, False)
    near_rest = [lax.ppermute(piece, ("h", "c"), [(1, 3), (2, 0)]) for piece in near]
    near_rest[-1], far_rest[0] = lax.optimization_barrier((near_rest[-1], far_rest[0]))
    passed = [
        lax.ppermute(piece + rest, ("h", "c"), [(0, 1), (3, 2)])
        for piece, rest in zip(near, near_rest)
    ]
    kept = [jnp.where(flag[0] == 1, piece, 0.0) for piece in near]
    out = weigh(flag, (far, far_rest), 1, flops=int(1e9))
    return weigh(flag, (kept, near_rest, passed), 0, out), over[0] > 0


def body(spectra, valid):
    quick, over = coherence(gather_by_bin(spectra, valid))
    return lax.cond(
        over,
        lambda: coherence(sort_by_bin(spectra, valid))[0],
        lambda: quick,
    )


def solution(mesh):
    fine = Mesh(mesh.devices.reshape(4, 2, 2, 4, 4), ("y", "h", "c", "x", "l"))
    return jax.shard_map(
        body,
        mesh=fine,
        in_specs=(P(None, ("x", "l"), None, ("y", "h", "c")), P(("x", "l"))),
        out_specs=P(None, ("x", "l"), ("y", "h", "c"), None),
        check_vma=False,
    )
```

```python
import jax
import jax.numpy as jnp
from jax import lax
from jax.experimental import pallas as pl
from jax.experimental.pallas import tpu as pltpu
from jax.sharding import Mesh, PartitionSpec as P

PLANE = ("h", "x", "l")
NEAR_CUTS = (128,)
STEPS = 1
SAVED = 8
MARK = 1e6
EXTRA = 8
VMEM_BYTES = 121 * 512 * 1024


def sort_kernel(valid_ref, x_ref, out_ref, rows_ref, sorted_ref, mask_ref, in_sems, out_sems):
    parts, windows, _, chans = x_ref.shape
    groups = in_sems.shape[1]
    rows, half = windows // groups, windows // 2

    def fetch(part, group):
        span = pl.ds(group * rows, rows)
        return pltpu.make_async_copy(
            x_ref.at[part, span], rows_ref.at[part, span], in_sems.at[part, group]
        )

    def store(part, group):
        side, first = divmod(group * rows, half)
        span = pl.ds(first, rows)
        return pltpu.make_async_copy(
            sorted_ref.at[side, :, part, span],
            out_ref.at[side, :, part, span],
            out_sems.at[part, group],
        )

    steps = [(part, group) for part in range(parts) for group in range(groups)]
    for step in steps:
        fetch(*step).start()
    lanes = mask_ref.shape[1]
    keep = valid_ref[...].astype(jnp.float32)
    mask_ref[...] = jnp.broadcast_to(keep, (lanes, windows)).T
    for part, group in steps:
        fetch(part, group).wait()
        for first in range(group * rows, (group + 1) * rows, 8):
            mask = mask_ref[first:first + 8, :]
            block = jnp.swapaxes(rows_ref[part, first:first + 8], 0, 1)
            side, at = divmod(first, half)
            for lane in range(0, chans, lanes):
                sorted_ref[side, :, part, at:at + 8, lane:lane + lanes] = (
                    block[:, :, lane:lane + lanes] * mask
                )
        store(part, group).start()
    for step in steps:
        store(*step).wait()


def sort_by_bin(spectra, valid):
    parts, windows, bins, chans = spectra.shape
    groups = 4
    shape = (2, bins, parts, windows // 2, chans)
    return pl.pallas_call(
        sort_kernel,
        out_shape=jax.ShapeDtypeStruct(shape, jnp.float32),
        in_specs=[
            pl.BlockSpec(memory_space=pltpu.VMEM),
            pl.BlockSpec(memory_space=pl.ANY),
        ],
        out_specs=pl.BlockSpec(memory_space=pl.ANY),
        scratch_shapes=[
            pltpu.VMEM(spectra.shape, jnp.float32),
            pltpu.VMEM(shape, jnp.float32),
            pltpu.VMEM((windows, 128), jnp.float32),
            pltpu.SemaphoreType.DMA((parts, groups)),
            pltpu.SemaphoreType.DMA((parts, groups)),
        ],
        compiler_params=pltpu.CompilerParams(vmem_limit_bytes=VMEM_BYTES),
    )(valid.reshape(1, windows), spectra)


def gather_kernel(valid_ref, x_ref, out_ref, rows_ref, sorted_ref, order_ref, in_sems, out_sems):
    parts, windows, _, chans = x_ref.shape
    groups = in_sems.shape[1]
    size = sorted_ref.shape[3]

    def fetch(part, group):
        span = pl.ds(group * (windows // groups), windows // groups)
        return pltpu.make_async_copy(
            x_ref.at[part, span], rows_ref.at[part, span], in_sems.at[part, group]
        )

    def store(part, side):
        return pltpu.make_async_copy(
            sorted_ref.at[side, :, part], out_ref.at[side, :, part], out_sems.at[part, side]
        )

    for part in range(parts):
        for group in range(groups):
            fetch(part, group).start()

    def place(at, count):
        order_ref[count] = at
        return count + valid_ref[0, at]

    count = lax.fori_loop(0, windows, place, jnp.int32(0), unroll=16)
    def pick(slot):
        return jnp.where(slot < count, order_ref[slot], 0)

    mark = jnp.where(count > 2 * size, MARK, 0.0)
    for part in range(parts):
        for group in range(groups):
            fetch(part, group).wait()
        for side in range(2):
            held = count - side * size
            for first in range(0, size, 8):
                rows = [
                    rows_ref[part, pick(side * size + first + at)] for at in range(8)
                ]
                block = jnp.swapaxes(jnp.stack(rows), 0, 1)
                row = lax.broadcasted_iota(jnp.int32, block.shape, 1) + first
                block = jnp.where(row < held, block, 0.0)
                if part == 0 and first + 8 == size:
                    block += jnp.where(row == size - 1, mark, 0.0)
                sorted_ref[side, :, part, first:first + 8] = block
            store(part, side).start()
    for part in range(parts):
        for side in range(2):
            store(part, side).wait()


def gather_by_bin(spectra, valid):
    parts, windows, bins, chans = spectra.shape
    groups, size = 2, windows // 2 - SAVED
    shape = (2, bins, parts, size, chans)
    return pl.pallas_call(
        gather_kernel,
        out_shape=jax.ShapeDtypeStruct(shape, jnp.float32),
        in_specs=[
            pl.BlockSpec(memory_space=pltpu.SMEM),
            pl.BlockSpec(memory_space=pl.ANY),
        ],
        out_specs=pl.BlockSpec(memory_space=pl.ANY),
        scratch_shapes=[
            pltpu.VMEM(spectra.shape, jnp.float32),
            pltpu.VMEM(shape, jnp.float32),
            pltpu.SMEM((windows,), jnp.int32),
            pltpu.SemaphoreType.DMA((parts, groups)),
            pltpu.SemaphoreType.DMA((parts, 2)),
        ],
        compiler_params=pltpu.CompilerParams(vmem_limit_bytes=VMEM_BYTES),
    )(valid.reshape(1, windows), spectra)


def halves(value):
    high = value.astype(jnp.bfloat16)
    return high, (value - high.astype(jnp.float32)).astype(jnp.bfloat16)


def dot(left, right):
    return lax.dot_general(
        left, right, (((0,), (0,)), ((), ())), preferred_element_type=jnp.float32
    )


def with_turned(right, windows):
    turned = []
    for at in range(0, right.shape[0], 2 * windows):
        turned += [-right[at + windows:at + 2 * windows], right[at:at + windows]]
    return jnp.concatenate([right, jnp.concatenate(turned, axis=0)], axis=1)


def tile_kernel(cuts, rows, copies, index_ref, left_ref, right_ref, *refs):
    del index_ref
    out_refs = refs[:len(cuts) - 1]
    _, sources, _, windows, chans = left_ref.shape
    first_step = pl.program_id(0) == 0
    if copies:
        refs[-2][...] = right_ref[...]
        last_slot = left_ref.shape[3] - 1
        largest = jnp.maximum(left_ref[0, :, 0, last_slot], right_ref[0, :, 0, last_slot])
        over = (jnp.max(largest[:, :128]) > 0.5 * MARK).astype(jnp.int32)
        refs[-1][0] = jnp.where(first_step, over, jnp.maximum(refs[-1][0], over))
    left = left_ref[0].reshape(-1, chans)
    right = right_ref[0].reshape(-1, chans)
    left_high, left_low = halves(left[:, chans - rows:])
    right_high, right_low = halves(with_turned(right, windows))
    tile = dot(left_high, right_low) + dot(left_low, right_high) + dot(left_high, right_high)
    energy = jnp.concatenate(
        [jnp.sum((side * side).reshape(-1, EXTRA, chans), axis=0) for side in (left, right)],
        axis=1,
    )

    @pl.when(first_step)
    def _():
        for ref, first, last in zip(out_refs, cuts, cuts[1:]):
            ref[:min(last, rows) - first] = tile[first:min(last, rows)]
        out_refs[-1][rows - cuts[-2]:] = energy

    @pl.when(jnp.logical_not(first_step))
    def _():
        for ref, first, last in zip(out_refs, cuts, cuts[1:]):
            ref[:min(last, rows) - first] += tile[first:min(last, rows)]
        out_refs[-1][rows - cuts[-2]:] += energy


def top_kernel(index_ref, left_ref, right_ref, out_ref):
    del index_ref
    windows, chans = right_ref.shape[3:]
    left_high, left_low = halves(left_ref[0].reshape(-1, left_ref.shape[-1]))
    right_high, right_low = halves(with_turned(right_ref[0].reshape(-1, chans), windows))
    out_ref[...] = (
        dot(left_high, right_low) + dot(left_low, right_high) + dot(left_high, right_high)
    )


def top_tile(left, right, index):
    _, sources, parts, windows, chans = left.shape
    shape = (chans // 2, 2 * chans)
    block = (1, sources, parts, windows)
    return pl.pallas_call(
        top_kernel,
        out_shape=jax.ShapeDtypeStruct(shape, jnp.float32),
        grid_spec=pltpu.PrefetchScalarGridSpec(
            num_scalar_prefetch=1,
            grid=(1,),
            in_specs=[
                pl.BlockSpec((*block, chans // 2), lambda k, index: (index[0], 0, 0, 0, 0)),
                pl.BlockSpec((*block, chans), lambda k, index: (index[1], 0, 0, 0, 0)),
            ],
            out_specs=pl.BlockSpec(shape, lambda k, index: (0, 0)),
        ),
        compiler_params=pltpu.CompilerParams(vmem_limit_bytes=32 * 1024 * 1024),
        cost_estimate=pl.CostEstimate(flops=1000, bytes_accessed=1000, transcendentals=0),
    )(index, left, right)


def cross_tile(left, right, index, cuts, same):
    _, sources, parts, windows, chans = left.shape
    rows = chans // 2 if same else chans
    cuts = [0, *cuts, rows + EXTRA]
    group = sources // STEPS
    block = (1, group, parts, windows, chans)
    outs = [
        jax.ShapeDtypeStruct((last - first, 2 * chans), jnp.float32)
        for first, last in zip(cuts, cuts[1:])
    ]
    specs = [pl.BlockSpec(out.shape, lambda k, index: (0, 0)) for out in outs]
    if same:
        outs.append(jax.ShapeDtypeStruct((1,) + right.shape[1:], jnp.float32))
        specs.append(pl.BlockSpec(block, lambda k, index: (0, k, 0, 0, 0)))
        outs.append(jax.ShapeDtypeStruct((1,), jnp.int32))
        specs.append(pl.BlockSpec(memory_space=pltpu.SMEM))
    return pl.pallas_call(
        lambda *refs: tile_kernel(cuts, rows, same, *refs),
        out_shape=outs,
        grid_spec=pltpu.PrefetchScalarGridSpec(
            num_scalar_prefetch=1,
            grid=(STEPS,),
            in_specs=[
                pl.BlockSpec(block, lambda k, index: (index[0], k, 0, 0, 0)),
                pl.BlockSpec(block, lambda k, index: (index[1], k, 0, 0, 0)),
            ],
            out_specs=specs,
        ),
        compiler_params=pltpu.CompilerParams(vmem_limit_bytes=32 * 1024 * 1024),
        cost_estimate=pl.CostEstimate(flops=1000, bytes_accessed=1000, transcendentals=0),
    )(index, left, right)


def weigh_kernel(adds, flag_ref, *refs):
    ins, out_ref = refs[:-1], refs[-1]
    chans = out_ref.shape[2]
    direct = flag_ref[0] == 1
    half = len(ins) // adds
    total = jnp.concatenate([sum(ref[...] for ref in ins[at::half]) for at in range(half)], axis=0)
    energy = jnp.sum(total[chans:], axis=0, keepdims=True)
    scale = 1.0 / jnp.sqrt(energy + 1e-06)
    down = jnp.broadcast_to(scale[:, :chans], (chans, chans)).T
    weight = down * scale[:, chans:]
    real = total[:chans, :chans] * weight
    imag = total[:chans, chans:] * weight

    @pl.when(direct)
    def _():
        out_ref[0, 0, :, :chans] = real
        out_ref[0, 0, :, chans:] = imag

    @pl.when(jnp.logical_not(direct))
    def _():
        out_ref[0, 0, :, :chans] = real.T
        out_ref[0, 0, :, chans:] = -imag.T


def weigh(flag, groups, step, onto=None, flops=1000):
    arrays = [piece for group in groups for piece in group]
    width = arrays[0].shape[1]
    kernel = lambda *refs: weigh_kernel(len(groups), *refs)
    extra = []
    if onto is not None:
        kernel = lambda *refs: weigh_kernel(len(groups), refs[0], *refs[2:])
        extra = [onto]
    return pl.pallas_call(
        kernel,
        out_shape=jax.ShapeDtypeStruct((2, 1, width // 2, width), jnp.float32),
        grid=(1,),
        in_specs=[pl.BlockSpec(memory_space=pltpu.SMEM)]
        + [pl.BlockSpec(memory_space=pl.ANY)] * len(extra)
        + [pl.BlockSpec(memory_space=pltpu.VMEM)] * len(arrays),
        out_specs=pl.BlockSpec((1, 1, width // 2, width), lambda k: (step, 0, 0, 0)),
        input_output_aliases={1: 0} if extra else {},
        compiler_params=pltpu.CompilerParams(vmem_limit_bytes=32 * 1024 * 1024),
        cost_estimate=pl.CostEstimate(flops=flops, bytes_accessed=1000, transcendentals=0),
    )(flag, *extra, *arrays)


def coherence(sent):
    high = lax.axis_index("h")
    core = lax.axis_index("c")
    index = jnp.stack([core, 1 - core]).astype(jnp.int32)
    index_one = jnp.stack([core, jnp.int32(0)]).astype(jnp.int32)
    flag = (high == core).astype(jnp.int32).reshape(1)
    _, bins, parts, windows, chans = sent.shape
    sent = sent.reshape(2 * bins, parts, windows, chans)
    got = lax.all_to_all(sent, PLANE, 0, 0, tiled=True)
    got = got.reshape(2, bins, parts, windows, chans)
    low, away, over = cross_tile(got, got, index, (), True)
    other = lax.ppermute(away, "c", [(0, 1), (1, 0)])
    low_rest = lax.ppermute(low, "h", [(0, 1), (1, 0)])
    near = cross_tile(got, other, index_one, NEAR_CUTS, False)
    top = top_tile(got, got, index)
    top_rest = lax.ppermute(top, "h", [(0, 1), (1, 0)])
    near_rest = [lax.ppermute(piece, ("h", "c"), [(1, 3), (2, 0)]) for piece in near]
    near_rest[-1], low_rest = lax.optimization_barrier((near_rest[-1], low_rest))
    passed = [
        lax.ppermute(piece + rest, ("h", "c"), [(0, 1), (3, 2)])
        for piece, rest in zip(near, near_rest)
    ]
    kept = [jnp.where(flag[0] == 1, piece, 0.0) for piece in near]
    out = weigh(flag, ([top, low], [top_rest, low_rest]), 1, flops=int(1e9))
    return weigh(flag, (kept, near_rest, passed), 0, out), over[0] > 0


def body(spectra, valid):
    quick, over = coherence(gather_by_bin(spectra, valid))
    return lax.cond(
        over,
        lambda: coherence(sort_by_bin(spectra, valid))[0],
        lambda: quick,
    )


def solution(mesh):
    fine = Mesh(mesh.devices.reshape(4, 2, 2, 4, 4), ("y", "h", "c", "x", "l"))
    return jax.shard_map(
        body,
        mesh=fine,
        in_specs=(P(None, ("x", "l"), None, ("y", "h", "c")), P(("x", "l"))),
        out_specs=P(None, ("x", "l"), ("y", "h", "c"), None),
        check_vma=False,
    )
```

```python
import jax
import jax.numpy as jnp
from jax import lax
from jax.experimental import pallas as pl
from jax.experimental.pallas import tpu as pltpu
from jax.sharding import Mesh, PartitionSpec as P

PLANE = ("h", "x", "l")
NEAR_CUTS = (128,)
STEPS = 1
SAVED = 8
MARK = 1e6
EXTRA = 8
VMEM_BYTES = 121 * 512 * 1024


def sort_kernel(valid_ref, x_ref, out_ref, rows_ref, sorted_ref, mask_ref, in_sems, out_sems):
    parts, windows, _, chans = x_ref.shape
    groups = in_sems.shape[1]
    rows, half = windows // groups, windows // 2

    def fetch(part, group):
        span = pl.ds(group * rows, rows)
        return pltpu.make_async_copy(
            x_ref.at[part, span], rows_ref.at[part, span], in_sems.at[part, group]
        )

    def store(part, group):
        side, first = divmod(group * rows, half)
        span = pl.ds(first, rows)
        return pltpu.make_async_copy(
            sorted_ref.at[side, :, part, span],
            out_ref.at[side, :, part, span],
            out_sems.at[part, group],
        )

    steps = [(part, group) for part in range(parts) for group in range(groups)]
    for step in steps:
        fetch(*step).start()
    lanes = mask_ref.shape[1]
    keep = valid_ref[...].astype(jnp.float32)
    mask_ref[...] = jnp.broadcast_to(keep, (lanes, windows)).T
    for part, group in steps:
        fetch(part, group).wait()
        for first in range(group * rows, (group + 1) * rows, 8):
            mask = mask_ref[first:first + 8, :]
            block = jnp.swapaxes(rows_ref[part, first:first + 8], 0, 1)
            side, at = divmod(first, half)
            for lane in range(0, chans, lanes):
                sorted_ref[side, :, part, at:at + 8, lane:lane + lanes] = (
                    block[:, :, lane:lane + lanes] * mask
                )
        store(part, group).start()
    for step in steps:
        store(*step).wait()


def sort_by_bin(spectra, valid):
    parts, windows, bins, chans = spectra.shape
    groups = 4
    shape = (2, bins, parts, windows // 2, chans)
    return pl.pallas_call(
        sort_kernel,
        out_shape=jax.ShapeDtypeStruct(shape, jnp.float32),
        in_specs=[
            pl.BlockSpec(memory_space=pltpu.VMEM),
            pl.BlockSpec(memory_space=pl.ANY),
        ],
        out_specs=pl.BlockSpec(memory_space=pl.ANY),
        scratch_shapes=[
            pltpu.VMEM(spectra.shape, jnp.float32),
            pltpu.VMEM(shape, jnp.float32),
            pltpu.VMEM((windows, 128), jnp.float32),
            pltpu.SemaphoreType.DMA((parts, groups)),
            pltpu.SemaphoreType.DMA((parts, groups)),
        ],
        compiler_params=pltpu.CompilerParams(vmem_limit_bytes=VMEM_BYTES),
    )(valid.reshape(1, windows), spectra)


def gather_kernel(valid_ref, x_ref, out_ref, rows_ref, sorted_ref, order_ref, in_sems, out_sems):
    parts, windows, _, chans = x_ref.shape
    groups = in_sems.shape[1]
    size = sorted_ref.shape[3]

    def fetch(part, group):
        span = pl.ds(group * (windows // groups), windows // groups)
        return pltpu.make_async_copy(
            x_ref.at[part, span], rows_ref.at[part, span], in_sems.at[part, group]
        )

    cuts = (0, size // 16 * 8, size)

    def store(part, side, piece):
        span = pl.ds(cuts[piece], cuts[piece + 1] - cuts[piece])
        return pltpu.make_async_copy(
            sorted_ref.at[side, :, part, span],
            out_ref.at[side, :, part, span],
            out_sems.at[part, side, piece],
        )

    for part in range(parts):
        for group in range(groups):
            fetch(part, group).start()

    def place(at, count):
        order_ref[count] = at
        return count + valid_ref[0, at]

    count = lax.fori_loop(0, windows, place, jnp.int32(0), unroll=16)
    def pick(slot):
        return jnp.where(slot < count, order_ref[slot], 0)

    mark = jnp.where(count > 2 * size, MARK, 0.0)
    for part in range(parts):
        for group in range(groups):
            fetch(part, group).wait()
        for side in range(2):
            held = count - side * size
            for first in range(0, size, 8):
                rows = [
                    rows_ref[part, pick(side * size + first + at)] for at in range(8)
                ]
                block = jnp.swapaxes(jnp.stack(rows), 0, 1)
                row = lax.broadcasted_iota(jnp.int32, block.shape, 1) + first
                block = jnp.where(row < held, block, 0.0)
                if part == 0 and first + 8 == size:
                    block += jnp.where(row == size - 1, mark, 0.0)
                sorted_ref[side, :, part, first:first + 8] = block
                if first + 8 in cuts:
                    store(part, side, cuts.index(first + 8) - 1).start()
    for part in range(parts):
        for side in range(2):
            for piece in range(2):
                store(part, side, piece).wait()


def gather_by_bin(spectra, valid):
    parts, windows, bins, chans = spectra.shape
    groups, size = 2, windows // 2 - SAVED
    shape = (2, bins, parts, size, chans)
    return pl.pallas_call(
        gather_kernel,
        out_shape=jax.ShapeDtypeStruct(shape, jnp.float32),
        in_specs=[
            pl.BlockSpec(memory_space=pltpu.SMEM),
            pl.BlockSpec(memory_space=pl.ANY),
        ],
        out_specs=pl.BlockSpec(memory_space=pl.ANY),
        scratch_shapes=[
            pltpu.VMEM(spectra.shape, jnp.float32),
            pltpu.VMEM(shape, jnp.float32),
            pltpu.SMEM((windows,), jnp.int32),
            pltpu.SemaphoreType.DMA((parts, groups)),
            pltpu.SemaphoreType.DMA((parts, 2, 2)),
        ],
        compiler_params=pltpu.CompilerParams(vmem_limit_bytes=VMEM_BYTES),
    )(valid.reshape(1, windows), spectra)


def halves(value):
    high = value.astype(jnp.bfloat16)
    return high, (value - high.astype(jnp.float32)).astype(jnp.bfloat16)


def dot(left, right):
    return lax.dot_general(
        left, right, (((0,), (0,)), ((), ())), preferred_element_type=jnp.float32
    )


def with_turned(right, windows):
    turned = []
    for at in range(0, right.shape[0], 2 * windows):
        turned += [-right[at + windows:at + 2 * windows], right[at:at + windows]]
    return jnp.concatenate([right, jnp.concatenate(turned, axis=0)], axis=1)


def tile_kernel(cuts, rows, copies, index_ref, left_ref, right_ref, *refs):
    del index_ref
    out_refs = refs[:len(cuts) - 1]
    _, sources, _, windows, chans = left_ref.shape
    first_step = pl.program_id(0) == 0
    if copies:
        refs[-2][...] = right_ref[...]
        last_slot = left_ref.shape[3] - 1
        largest = jnp.maximum(left_ref[0, :, 0, last_slot], right_ref[0, :, 0, last_slot])
        over = (jnp.max(largest[:, :128]) > 0.5 * MARK).astype(jnp.int32)
        refs[-1][0] = jnp.where(first_step, over, jnp.maximum(refs[-1][0], over))
    left = left_ref[0].reshape(-1, chans)
    right = right_ref[0].reshape(-1, chans)
    left_high, left_low = halves(left[:, chans - rows:])
    right_high, right_low = halves(with_turned(right, windows))
    tile = dot(left_high, right_low) + dot(left_low, right_high) + dot(left_high, right_high)
    energy = jnp.concatenate(
        [jnp.sum((side * side).reshape(-1, EXTRA, chans), axis=0) for side in (left, right)],
        axis=1,
    )

    @pl.when(first_step)
    def _():
        for ref, first, last in zip(out_refs, cuts, cuts[1:]):
            ref[:min(last, rows) - first] = tile[first:min(last, rows)]
        out_refs[-1][rows - cuts[-2]:] = energy

    @pl.when(jnp.logical_not(first_step))
    def _():
        for ref, first, last in zip(out_refs, cuts, cuts[1:]):
            ref[:min(last, rows) - first] += tile[first:min(last, rows)]
        out_refs[-1][rows - cuts[-2]:] += energy


def top_kernel(index_ref, left_ref, right_ref, out_ref):
    del index_ref
    windows, chans = right_ref.shape[3:]
    left_high, left_low = halves(left_ref[0].reshape(-1, left_ref.shape[-1]))
    right_high, right_low = halves(with_turned(right_ref[0].reshape(-1, chans), windows))
    out_ref[...] = (
        dot(left_high, right_low) + dot(left_low, right_high) + dot(left_high, right_high)
    )


def top_tile(left, right, index):
    _, sources, parts, windows, chans = left.shape
    shape = (chans // 2, 2 * chans)
    block = (1, sources, parts, windows)
    return pl.pallas_call(
        top_kernel,
        out_shape=jax.ShapeDtypeStruct(shape, jnp.float32),
        grid_spec=pltpu.PrefetchScalarGridSpec(
            num_scalar_prefetch=1,
            grid=(1,),
            in_specs=[
                pl.BlockSpec((*block, chans // 2), lambda k, index: (index[0], 0, 0, 0, 0)),
                pl.BlockSpec((*block, chans), lambda k, index: (index[1], 0, 0, 0, 0)),
            ],
            out_specs=pl.BlockSpec(shape, lambda k, index: (0, 0)),
        ),
        compiler_params=pltpu.CompilerParams(vmem_limit_bytes=32 * 1024 * 1024),
        cost_estimate=pl.CostEstimate(flops=1000, bytes_accessed=1000, transcendentals=0),
    )(index, left, right)


def cross_tile(left, right, index, cuts, same):
    _, sources, parts, windows, chans = left.shape
    rows = chans // 2 if same else chans
    cuts = [0, *cuts, rows + EXTRA]
    group = sources // STEPS
    block = (1, group, parts, windows, chans)
    outs = [
        jax.ShapeDtypeStruct((last - first, 2 * chans), jnp.float32)
        for first, last in zip(cuts, cuts[1:])
    ]
    specs = [pl.BlockSpec(out.shape, lambda k, index: (0, 0)) for out in outs]
    if same:
        outs.append(jax.ShapeDtypeStruct((1,) + right.shape[1:], jnp.float32))
        specs.append(pl.BlockSpec(block, lambda k, index: (0, k, 0, 0, 0)))
        outs.append(jax.ShapeDtypeStruct((1,), jnp.int32))
        specs.append(pl.BlockSpec(memory_space=pltpu.SMEM))
    return pl.pallas_call(
        lambda *refs: tile_kernel(cuts, rows, same, *refs),
        out_shape=outs,
        grid_spec=pltpu.PrefetchScalarGridSpec(
            num_scalar_prefetch=1,
            grid=(STEPS,),
            in_specs=[
                pl.BlockSpec(block, lambda k, index: (index[0], k, 0, 0, 0)),
                pl.BlockSpec(block, lambda k, index: (index[1], k, 0, 0, 0)),
            ],
            out_specs=specs,
        ),
        compiler_params=pltpu.CompilerParams(vmem_limit_bytes=32 * 1024 * 1024),
        cost_estimate=pl.CostEstimate(flops=1000, bytes_accessed=1000, transcendentals=0),
    )(index, left, right)


def weigh_kernel(adds, flag_ref, *refs):
    ins, out_ref = refs[:-1], refs[-1]
    chans = out_ref.shape[2]
    direct = flag_ref[0] == 1
    half = len(ins) // adds
    total = jnp.concatenate([sum(ref[...] for ref in ins[at::half]) for at in range(half)], axis=0)
    energy = jnp.sum(total[chans:], axis=0, keepdims=True)
    scale = 1.0 / jnp.sqrt(energy + 1e-06)
    down = jnp.broadcast_to(scale[:, :chans], (chans, chans)).T
    weight = down * scale[:, chans:]
    real = total[:chans, :chans] * weight
    imag = total[:chans, chans:] * weight

    @pl.when(direct)
    def _():
        out_ref[0, 0, :, :chans] = real
        out_ref[0, 0, :, chans:] = imag

    @pl.when(jnp.logical_not(direct))
    def _():
        out_ref[0, 0, :, :chans] = real.T
        out_ref[0, 0, :, chans:] = -imag.T


def weigh(flag, groups, step, onto=None, flops=1000):
    arrays = [piece for group in groups for piece in group]
    width = arrays[0].shape[1]
    kernel = lambda *refs: weigh_kernel(len(groups), *refs)
    extra = []
    if onto is not None:
        kernel = lambda *refs: weigh_kernel(len(groups), refs[0], *refs[2:])
        extra = [onto]
    return pl.pallas_call(
        kernel,
        out_shape=jax.ShapeDtypeStruct((2, 1, width // 2, width), jnp.float32),
        grid=(1,),
        in_specs=[pl.BlockSpec(memory_space=pltpu.SMEM)]
        + [pl.BlockSpec(memory_space=pl.ANY)] * len(extra)
        + [pl.BlockSpec(memory_space=pltpu.VMEM)] * len(arrays),
        out_specs=pl.BlockSpec((1, 1, width // 2, width), lambda k: (step, 0, 0, 0)),
        input_output_aliases={1: 0} if extra else {},
        compiler_params=pltpu.CompilerParams(vmem_limit_bytes=32 * 1024 * 1024),
        cost_estimate=pl.CostEstimate(flops=flops, bytes_accessed=1000, transcendentals=0),
    )(flag, *extra, *arrays)


def coherence(sent):
    high = lax.axis_index("h")
    core = lax.axis_index("c")
    index = jnp.stack([core, 1 - core]).astype(jnp.int32)
    index_one = jnp.stack([core, jnp.int32(0)]).astype(jnp.int32)
    flag = (high == core).astype(jnp.int32).reshape(1)
    _, bins, parts, windows, chans = sent.shape
    sent = sent.reshape(2 * bins, parts, windows, chans)
    got = lax.all_to_all(sent, PLANE, 0, 0, tiled=True)
    got = got.reshape(2, bins, parts, windows, chans)
    low, away, over = cross_tile(got, got, index, (), True)
    other = lax.ppermute(away, "c", [(0, 1), (1, 0)])
    low_rest = lax.ppermute(low, "h", [(0, 1), (1, 0)])
    near = cross_tile(got, other, index_one, NEAR_CUTS, False)
    top = top_tile(got, got, index)
    top_rest = lax.ppermute(top, "h", [(0, 1), (1, 0)])
    near_rest = [lax.ppermute(piece, ("h", "c"), [(1, 3), (2, 0)]) for piece in near]
    near_rest[-1], low_rest = lax.optimization_barrier((near_rest[-1], low_rest))
    passed = [
        lax.ppermute(piece + rest, ("h", "c"), [(0, 1), (3, 2)])
        for piece, rest in zip(near, near_rest)
    ]
    kept = [jnp.where(flag[0] == 1, piece, 0.0) for piece in near]
    out = weigh(flag, ([top, low], [top_rest, low_rest]), 1, flops=int(1e9))
    return weigh(flag, (kept, near_rest, passed), 0, out), over[0] > 0


def body(spectra, valid):
    quick, over = coherence(gather_by_bin(spectra, valid))
    return lax.cond(
        over,
        lambda: coherence(sort_by_bin(spectra, valid))[0],
        lambda: quick,
    )


def solution(mesh):
    fine = Mesh(mesh.devices.reshape(4, 2, 2, 4, 4), ("y", "h", "c", "x", "l"))
    return jax.shard_map(
        body,
        mesh=fine,
        in_specs=(P(None, ("x", "l"), None, ("y", "h", "c")), P(("x", "l"))),
        out_specs=P(None, ("x", "l"), ("y", "h", "c"), None),
        check_vma=False,
    )
```
